512 devices in a mesh: dp: 16 (over x, y), tensor: 32 (over z, core).
Axes of the slice: x: 4, y: 4, z: 16, core: 2. Of those that a mesh axis runs over, the one named last changes fastest.
Arguments:
- tokens: bfloat16 [2048, 4096], P('dp', 'tensor'), may hold values from -6 to 6
- w_in: bfloat16 [4096, 8192], P('dp', 'tensor'), may hold values from -0.09375 to 0.09375
- conv_weight: float32 [4, 8192], P(None, 'tensor'), may hold values from -3 to 3
- w_dtlow: bfloat16 [8192, 512], P('tensor'), may hold values from -0.0625 to 0.0625
- w_bc: bfloat16 [8192, 32], P('tensor'), may hold values from -0.0625 to 0.0625
- w_dt: bfloat16 [512, 8192], P(None, 'tensor'), may hold values from -0.25 to 0.25
- dt_bias: float32 [8192], P('tensor'), may hold values from -4 to -1
- a_log: float32 [8192, 16], P('tensor'), may hold values from -3 to 0.7
- d_skip: float32 [8192], P('tensor'), may hold values from 0.5 to 2
- w_out: bfloat16 [8192, 4096], P('tensor', 'dp'), may hold values from -0.0625 to 0.0625
- cotangent: bfloat16 [2048, 4096], P('dp', 'tensor'), may hold values from -6 to 6
- err_in: float32 [4096, 8192], P('dp', 'tensor'), may hold values from -1.8 to 1.8
- err_out: float32 [8192, 4096], P('tensor', 'dp'), may hold values from -1.8 to 1.8
Outputs:
- mixed: bfloat16 [2048, 4096], P('dp', 'tensor')
- input_grad: bfloat16 [2048, 4096], P('dp', 'tensor')
- update_in: float32 [4096, 8192], P('dp', 'tensor')
- residue_in: float32 [4096, 8192], P('dp', 'tensor')
- update_out: float32 [8192, 4096], P('tensor', 'dp')
- residue_out: float32 [8192, 4096], P('tensor', 'dp')
The draws below stay inside these ranges and needn't reach their ends.
All inputs are finite; a program needn't handle non-finite values. Where the reference program divides by a largest or mean magnitude, that divisor is 1e-20 or more.
Results may differ from the reference program's by a relative error of at most 0.035.
Values may be sent and summed in bfloat16 or wider, within the bound.
No kernel may reach another device: no remote copies, remote signals or barrier semaphores. Data moves between devices by JAX's collectives and lax.ppermute only.
A program may use at most 128 MiB of HBM per device.

```python
import jax
import jax.numpy as jnp
from jax import lax

D = 4096
DI = 8192
N = 16
R = 512
KC = 4
QB = 128
TOK = 128
TOKENS = 2048
CH = 256
N_DP = 16
N_TENSOR = 32


def shard_levels(stream_key, shape, split, least, top_value):
    gain = 1.0
    for position, blocks in split:
        steps = jax.random.uniform(jax.random.fold_in(jax.random.fold_in(stream_key, 6), position), (blocks,), jnp.float32, least / len(split), top_value / len(split))
        gain = gain * jnp.repeat(jnp.exp(steps), shape[position] // blocks).reshape((-1,) + (1,) * (len(shape) - 1 - position))
    return gain


def noise(rng, extent, scale, bound, split=(), kind=jnp.bfloat16):
    array = scale * jax.random.normal(rng, extent, jnp.float32)
    if split:
        array = array * shard_levels(rng, extent, split, -0.22, 0.18)
    return jnp.clip(array, -bound, bound).astype(kind)


def setup_inputs(seed: int = 0) -> dict:
    splits = jax.random.split(jax.random.key(seed), 14)
    return {
        "tokens": noise(splits[0], (TOKENS, D), 1.0, 6.0, ((0, 16), (1, 32))),
        "w_in": noise(splits[1], (D, DI), D ** -0.5, 0.09375, ((0, 16), (1, 32))),
        "conv_weight": noise(splits[2], (KC, DI), 0.5, 3.0, ((1, 32),), jnp.float32),
        "w_dtlow": noise(splits[3], (DI, R), DI ** -0.5, 0.0625, ((0, 32),)),
        "w_bc": noise(splits[4], (DI, 2 * N), DI ** -0.5, 0.0625, ((0, 32),)),
        "w_dt": noise(splits[5], (R, DI), R ** -0.5, 0.25, ((1, 32),)),
        "dt_bias": jnp.clip(-4.0 + 3.0 * jax.random.uniform(splits[6], (DI,), jnp.float32) ** shard_levels(splits[6], (DI,), ((0, 32),), -0.2, 0.2), -4.0, -1.0),
        "a_log": jnp.clip(-3.0 + 3.7 * jax.random.uniform(splits[7], (DI, N), jnp.float32) ** shard_levels(splits[7], (DI, N), ((0, 32),), -0.2, 0.2), -3.0, 0.7),
        "d_skip": jnp.clip(0.5 + 1.5 * jax.random.uniform(splits[8], (DI,), jnp.float32) ** shard_levels(splits[8], (DI,), ((0, 32),), -0.2, 0.2), 0.5, 2.0),
        "w_out": noise(splits[9], (DI, D), DI ** -0.5, 0.0625, ((0, 32), (1, 16))),
        "cotangent": noise(splits[10], (TOKENS, D), 1.0, 6.0, ((0, 16), (1, 32))),
        "err_in": noise(splits[11], (D, DI), 0.3, 1.8, ((0, 16), (1, 32)), jnp.float32),
        "err_out": noise(splits[12], (DI, D), 0.3, 1.8, ((0, 32), (1, 16)), jnp.float32),
    }


eps_scale = 1e-06

def conv_silu(inner_f, conv_weight):
    kernel_width = conv_weight.shape[0]
    length = inner_f.shape[0]
    padded = jnp.concatenate([jnp.zeros((kernel_width - 1, inner_f.shape[1]), inner_f.dtype), inner_f], axis=0)
    summed = jnp.zeros_like(inner_f)
    for offset in range(kernel_width):
        summed = summed + conv_weight[offset][None, :] * padded[offset:offset + length]
    return jax.nn.silu(summed)

def ssm_scan(conv_f, delta, bmat, cmat, a_neg, d_skip):

    def advance(state, inputs):
        token_x, token_delta, token_b, token_c = inputs
        state = jnp.exp(token_delta[:, None] * a_neg) * state + (token_delta * token_x)[:, None] * token_b[None, :]
        output = lax.optimization_barrier(jnp.sum(state * token_c[None, :], axis=1)) + d_skip * token_x
        return (state, output)
    initial = jnp.zeros(a_neg.shape, conv_f.dtype)
    _, outputs = lax.scan(advance, initial, (conv_f, delta, bmat, cmat))
    return outputs

def block_sum(parts, block_size):
    groups, row_count, col_count = parts.shape
    blocks = parts.reshape(groups, row_count, col_count // block_size, block_size)
    scales = (lax.optimization_barrier(jnp.max(jnp.abs(blocks), axis=-1, keepdims=True)) + eps_scale).astype(jnp.bfloat16)
    scales = lax.optimization_barrier(scales).astype(jnp.float32)
    coded = (blocks / scales).astype(jnp.bfloat16)
    coded = lax.optimization_barrier(coded).astype(jnp.float32)
    summed = lax.optimization_barrier(jnp.sum(coded * scales, axis=0))
    return summed.reshape(row_count, col_count).astype(jnp.bfloat16)

def soft_sign(grad, block_size):
    row_count, col_count = grad.shape
    blocks = grad.reshape(row_count, col_count // block_size, block_size)
    mean_abs = lax.optimization_barrier(jnp.mean(jnp.abs(blocks), axis=-1, keepdims=True)) + eps_scale
    return jnp.tanh(blocks / mean_abs).reshape(row_count, col_count).astype(jnp.bfloat16)

def contract(left, right, left_dim, right_dim):
    return lax.dot_general(left, right, (((left_dim,), (right_dim,)), ((), ())), preferred_element_type=jnp.float32)

def reference(tokens, w_in, conv_weight, w_dtlow, w_bc, w_dt, dt_bias, a_log, d_skip, w_out, cotangent, err_in, err_out):
    a_neg = -jnp.exp(a_log)
    groups = N_TENSOR

    def replica(carry, pair):
        vote_in, vote_out = carry
        seq_tokens, seq_cot = pair
        inner = jnp.dot(seq_tokens, w_in, preferred_element_type=jnp.float32).astype(jnp.bfloat16)
        inner_f = lax.optimization_barrier(inner).astype(jnp.float32)
        conv_f, conv_back = jax.vjp(lambda value: conv_silu(value, conv_weight), inner_f)
        conv_out = lax.optimization_barrier(conv_f.astype(jnp.bfloat16))
        delta_low = jnp.dot(conv_out, w_dtlow, preferred_element_type=jnp.float32).astype(jnp.bfloat16)
        state_proj = jnp.dot(conv_out, w_bc, preferred_element_type=jnp.float32)
        delta_pre = jnp.dot(delta_low, w_dt, preferred_element_type=jnp.float32) + dt_bias
        delta = jax.nn.softplus(delta_pre)
        bmat = state_proj[:, :N]
        cmat = state_proj[:, N:]
        conv_in = conv_out.astype(jnp.float32)
        ys, ssm_back = jax.vjp(lambda value, step, inmap, outmap: ssm_scan(value, step, inmap, outmap, a_neg, d_skip), conv_in, delta, bmat, cmat)
        hidden_out = ys.astype(jnp.bfloat16)
        out_parts = jnp.einsum('tgc,gcd->gtd', hidden_out.astype(jnp.float32).reshape(TOK, groups, CH), w_out.astype(jnp.float32).reshape(groups, CH, D))
        mixed = block_sum(out_parts, QB)
        grad_out = contract(hidden_out, seq_cot, 0, 0)
        d_hidden = contract(seq_cot, w_out, 1, 1)
        d_conv, d_delta, d_bmat, d_cmat = ssm_back(d_hidden)
        d_pre = (d_delta * jax.nn.sigmoid(delta_pre)).astype(jnp.bfloat16)
        d_low = contract(d_pre, w_dt, 1, 1).astype(jnp.bfloat16)
        d_state = jnp.concatenate([d_bmat, d_cmat], axis=1).astype(jnp.bfloat16)
        d_conv_all = d_conv + contract(d_low, w_dtlow, 1, 1) + contract(d_state, w_bc, 1, 1)
        d_inner_f, = conv_back(d_conv_all)
        d_inner = d_inner_f.astype(jnp.bfloat16)
        grad_in = contract(seq_tokens, d_inner, 0, 0)
        grad_parts = jnp.einsum('tgc,dgc->gtd', d_inner.astype(jnp.float32).reshape(TOK, groups, CH), w_in.astype(jnp.float32).reshape(D, groups, CH))
        input_grad = block_sum(grad_parts, QB)
        vote_in = vote_in + soft_sign(grad_in, QB).astype(jnp.float32)
        vote_out = vote_out + soft_sign(grad_out, QB).astype(jnp.float32)
        return ((vote_in, vote_out), (mixed, input_grad))
    initial = (jnp.zeros((D, DI), jnp.float32), jnp.zeros((DI, D), jnp.float32))
    pairs = (tokens.reshape(N_DP, TOK, D), cotangent.reshape(N_DP, TOK, D))
    (vote_in, vote_out), (mixed, input_grad) = lax.scan(replica, initial, pairs)
    merged_in = vote_in / N_DP + err_in
    merged_out = vote_out / N_DP + err_out
    update_in = jnp.tanh(4.0 * merged_in)
    update_out = jnp.tanh(4.0 * merged_out)
    return (mixed.reshape(TOKENS, D), input_grad.reshape(TOKENS, D), update_in, merged_in - update_in, update_out, merged_out - update_out)
```

```python
import jax
import jax.numpy as jnp
from jax import lax
from jax.experimental import pallas as pl
from jax.experimental.pallas import tpu as pltpu
from jax.sharding import PartitionSpec as P

QB = 128


eps_scale = 1e-06


def contract(left, right, left_dim, right_dim):
    return lax.dot_general(
        left, right, (((left_dim,), (right_dim,)), ((), ())), preferred_element_type=jnp.float32
    )


def identity(size):
    rows = lax.broadcasted_iota(jnp.int32, (size, size), 0)
    cols = lax.broadcasted_iota(jnp.int32, (size, size), 1)
    return jnp.where(rows == cols, 1.0, 0.0).astype(jnp.bfloat16)


def scan_kernel(
    small_ref, w_dt_ref, bias_ref, a_neg_ref, skip_ref, conv_ref, dh_ref,
    hidden_ref, dconv_ref, back_ref,
    delta_s, x_s, u_s, y_s, dd_s, states,
):
    tokens, channels = conv_ref.shape
    n = a_neg_ref.shape[0]
    rank = w_dt_ref.shape[0]
    low = small_ref[:, :rank]
    pre = jnp.dot(low, w_dt_ref[...], preferred_element_type=jnp.float32) + bias_ref[...]
    delta = jax.nn.softplus(pre)
    x = conv_ref[...].astype(jnp.float32)
    delta_s[...] = delta
    x_s[...] = x
    u_s[...] = delta * x
    maps = contract(identity(2 * n), small_ref[:, rank:], 1, 1)
    a_neg = a_neg_ref[...]
    skip = skip_ref[...]
    states[0] = jnp.zeros((n, channels), jnp.float32)

    def columns(rolled, row, j):
        return jnp.broadcast_to(rolled[row : row + n, j : j + 1], (n, channels))

    def forward(chunk, h):
        start = pl.multiple_of(chunk * 8, 8)
        d8 = delta_s[pl.ds(start, 8), :]
        x8 = x_s[pl.ds(start, 8), :]
        u8 = u_s[pl.ds(start, 8), :]
        rolled = pltpu.roll(maps, lax.rem(tokens - start, tokens), 1)
        rows = []
        for j in range(8):
            h = jnp.exp(d8[j : j + 1] * a_neg) * h + u8[j : j + 1] * columns(rolled, 0, j)
            states[start + j + 1] = h
            rows.append(jnp.sum(h * columns(rolled, n, j), axis=0, keepdims=True))
        y_s[pl.ds(start, 8), :] = jnp.concatenate(rows, axis=0) + skip * x8
        return h

    lax.fori_loop(0, tokens // 8, forward, jnp.zeros((n, channels), jnp.float32))
    hidden_ref[...] = y_s[...].astype(hidden_ref.dtype)
    lane = lax.broadcasted_iota(jnp.int32, (n, tokens), 1)

    def backward(step, carry):
        g_next, acc_b, acc_c = carry
        start = pl.multiple_of(tokens - 8 - step * 8, 8)
        d8 = delta_s[pl.ds(start, 8), :]
        x8 = x_s[pl.ds(start, 8), :]
        u8 = u_s[pl.ds(start, 8), :]
        dy8 = dh_ref[pl.ds(start, 8), :]
        rolled = pltpu.roll(maps, lax.rem(tokens - start, tokens), 1)
        rows_a, rows_b = [None] * 8, [None] * 8
        for j in range(7, -1, -1):
            dy = dy8[j : j + 1]
            g = g_next + dy * columns(rolled, n, j)
            here = lane == start + j
            acc_c = jnp.where(here, jnp.sum(dy * states[start + j + 1], axis=1, keepdims=True), acc_c)
            acc_b = jnp.where(here, jnp.sum(g * u8[j : j + 1], axis=1, keepdims=True), acc_b)
            rows_b[j] = jnp.sum(g * columns(rolled, 0, j), axis=0, keepdims=True)
            g_next = g * jnp.exp(d8[j : j + 1] * a_neg)
            rows_a[j] = jnp.sum(g_next * (states[start + j] * a_neg), axis=0, keepdims=True)
        sum_b = jnp.concatenate(rows_b, axis=0)
        dd_s[pl.ds(start, 8), :] = jnp.concatenate(rows_a, axis=0) + x8 * sum_b
        dconv_ref[pl.ds(start, 8), :] = d8 * sum_b + skip * dy8
        return g_next, acc_b, acc_c

    zero = jnp.zeros((n, tokens), jnp.float32)
    _, acc_b, acc_c = lax.fori_loop(
        0, tokens // 8, backward, (jnp.zeros((n, channels), jnp.float32), zero, zero)
    )
    d_pre = (dd_s[...] * jax.nn.sigmoid(pre)).astype(jnp.bfloat16)
    back_ref[:, :rank] = contract(d_pre, w_dt_ref[...], 1, 1).astype(back_ref.dtype)
    both = jnp.concatenate([acc_b, acc_c], axis=0).astype(jnp.bfloat16)
    back_ref[:, rank:] = contract(identity(tokens), both, 1, 1).astype(back_ref.dtype)


VMEM_BYTES = 16 << 20


def local_call(kernel, shapes, scratch=(), specs=None):
    more = {} if specs is None else {"grid": (1,), "in_specs": specs}
    return pl.pallas_call(
        kernel,
        **more,
        out_shape=tuple(jax.ShapeDtypeStruct(shape, kind) for shape, kind in shapes),
        scratch_shapes=list(scratch),
        compiler_params=pltpu.CompilerParams(vmem_limit_bytes=VMEM_BYTES),
    )


def pair_kernel(keep_ref, give_ref, *refs):
    refs[-1][...] = (keep_ref[...].astype(jnp.float32) + give_ref[...].astype(jnp.float32)).astype(jnp.bfloat16)


def pairs_kernel(keep_out_ref, give_out_ref, keep_in_ref, give_in_ref, total_ref):
    rows = keep_out_ref.shape[1]
    out = keep_out_ref[...] + give_out_ref[...].astype(jnp.float32)
    total_ref[:, :rows, :] = out.astype(jnp.bfloat16)
    grad = keep_in_ref[...] + give_in_ref[...].astype(jnp.float32)
    total_ref[:, rows:, :] = grad.astype(jnp.bfloat16)


def share_kernel(parts_ref, *refs):
    total = jnp.sum(parts_ref[...].astype(jnp.float32), axis=0).astype(jnp.bfloat16)
    refs[-1][...] = jnp.broadcast_to(total[None], parts_ref.shape)


def pack_kernel(mine_ref, other_ref, block_ref, packed_ref):
    chips, height, lanes = packed_ref.shape
    rows, width = mine_ref.shape
    ahead = height - rows
    total = mine_ref[...].astype(jnp.float32) + other_ref[...].astype(jnp.float32)
    tiles = pl.cdiv(width, lanes)
    total = jnp.concatenate([total, jnp.zeros((rows, tiles * lanes - width), jnp.float32)], axis=1)
    share = total.reshape(chips, rows // chips, tiles * lanes)
    pieces = [share[:, :, i * lanes : (i + 1) * lanes] for i in range(tiles)]
    spare = ahead - tiles * (rows // chips)
    if spare:
        pieces.append(jnp.zeros((chips, spare, lanes), jnp.float32))
    packed_ref[:, :ahead, :] = jnp.concatenate(pieces, axis=1).astype(jnp.bfloat16)
    packed_ref[:, ahead:, :] = jnp.broadcast_to(block_ref[...][None], (chips, rows, lanes))


def unpack_kernel(parts_ref, after_ref, total_ref):
    _, height, width = total_ref.shape
    lanes = parts_ref.shape[2]
    total = jnp.sum(parts_ref[...].astype(jnp.float32), axis=0)
    pieces = [total[i * height : (i + 1) * height] for i in range(pl.cdiv(width, lanes))]
    total = jnp.concatenate(pieces, axis=1)[:, :width].astype(jnp.bfloat16)
    total_ref[...] = jnp.broadcast_to(total[None], total_ref.shape)


def in_order(even, mine, other):
    return jnp.concatenate([jnp.where(even, mine, other), jnp.where(even, other, mine)], axis=1)


def inner_kernel(
    mine_ref, other_ref, even_ref, w_in_ref, taps_ref, low_ref, bc_ref,
    whole_ref, pre_ref, conv_ref, small_ref, total_s,
):
    chips, rows, block = mine_ref.shape
    even = even_ref[...] > 0

    def step(chip, carry):
        features = in_order(even, mine_ref[chip], other_ref[chip])
        whole_ref[chip] = features
        total_s[...] += jnp.dot(features, w_in_ref[chip], preferred_element_type=jnp.float32)
        return carry

    total_s[...] = jnp.zeros_like(total_s)
    lax.fori_loop(0, chips, step, 0, unroll=4)
    inner = total_s[...].astype(jnp.bfloat16).astype(jnp.float32)
    taps = taps_ref[...]
    width = taps.shape[0]
    row = lax.broadcasted_iota(jnp.int32, inner.shape, 0)
    pre = taps[width - 1 :] * inner
    for back in range(1, width):
        shifted = jnp.where(row >= back, pltpu.roll(inner, back, 0), 0.0)
        pre = pre + taps[width - 1 - back : width - back] * shifted
    conv = (pre / (1.0 + jnp.exp(-pre))).astype(jnp.bfloat16)
    pre_ref[...] = pre
    conv_ref[...] = conv
    rank = low_ref.shape[1]
    small_ref[:, :rank] = jnp.dot(conv, low_ref[...], preferred_element_type=jnp.float32).astype(jnp.bfloat16)
    small_ref[:, rank:] = jnp.dot(conv, bc_ref[...], preferred_element_type=jnp.float32).astype(jnp.bfloat16)


def cotangent_kernel(mine_ref, other_ref, even_ref, w_out_ref, whole_ref, hidden_ref):
    chips = w_out_ref.shape[0]
    even = even_ref[...] > 0

    def step(chip, carry):
        features = in_order(even, mine_ref[chip], other_ref[chip])
        whole_ref[chip] = features
        hidden_ref[...] += contract(features, w_out_ref[chip], 1, 1)
        return carry

    hidden_ref[...] = jnp.zeros_like(hidden_ref)
    lax.fori_loop(0, chips, step, 0, unroll=4)


def coded(part):
    scale = (jnp.max(jnp.abs(part), axis=1, keepdims=True) + eps_scale).astype(jnp.bfloat16)
    scale = scale.astype(jnp.float32)
    return (part / scale).astype(jnp.bfloat16).astype(jnp.float32) * scale


def split_parts(even, part, keep_ref, give_ref, chip):
    first, second = coded(part[:, :QB]), coded(part[:, QB:])
    keep_ref[chip] = jnp.where(even, first, second)
    give_ref[chip] = jnp.where(even, second, first).astype(give_ref.dtype)


def soft_sign(grad):
    signs = []
    for start in range(0, grad.shape[1], QB):
        part = grad[:, start : start + QB]
        mean = jnp.mean(jnp.abs(part), axis=1, keepdims=True) + eps_scale
        signs.append(jnp.tanh(part / mean).astype(jnp.bfloat16))
    return jnp.concatenate(signs, axis=1)


def sign_out_kernel(hidden_ref, cot_ref, after_ref, sign_ref):
    hidden = hidden_ref[...]

    def step(chip, carry):
        sign_ref[chip] = soft_sign(contract(hidden, cot_ref[chip], 0, 0))
        return carry

    lax.fori_loop(0, cot_ref.shape[0], step, 0, unroll=2)


def out_kernel(hidden_ref, w_out_ref, even_ref, after_ref, keep_ref, give_ref):
    hidden = hidden_ref[...]
    even = even_ref[...] > 0

    def step(chip, carry):
        part = jnp.dot(hidden, w_out_ref[chip], preferred_element_type=jnp.float32)
        split_parts(even, part, keep_ref, give_ref, chip)
        return carry

    lax.fori_loop(0, w_out_ref.shape[0], step, 0, unroll=2)


def sign_in_kernel(
    back_ref, low_ref, bc_ref, d_conv_ref, pre_ref, taps_ref, whole_ref, d_inner_ref, sign_ref
):
    rank = low_ref.shape[1]
    back = back_ref[...]
    d_conv = (
        d_conv_ref[...]
        + contract(back[:, :rank], low_ref[...], 1, 1)
        + contract(back[:, rank:], bc_ref[...], 1, 1)
    )
    pre = pre_ref[...]
    gate = jax.nn.sigmoid(pre)
    d_sum = d_conv * (gate * (1.0 + pre * (1.0 - gate)))
    taps = taps_ref[...]
    width = taps.shape[0]
    rows = d_sum.shape[0]
    row = lax.broadcasted_iota(jnp.int32, d_sum.shape, 0)
    d_inner = taps[width - 1 :] * d_sum
    for ahead in range(1, width):
        shifted = jnp.where(row < rows - ahead, pltpu.roll(d_sum, rows - ahead, 0), 0.0)
        d_inner = d_inner + taps[width - 1 - ahead : width - ahead] * shifted
    d_inner = d_inner.astype(jnp.bfloat16)
    d_inner_ref[...] = d_inner

    def step(chip, carry):
        side = sign_ref.shape[0]
        sign_ref[lax.rem(chip, side), lax.div(chip, side)] = soft_sign(contract(whole_ref[chip], d_inner, 0, 0))
        return carry

    lax.fori_loop(0, whole_ref.shape[0], step, 0, unroll=2)


def grad_kernel(d_inner_ref, w_in_ref, even_ref, keep_ref, give_ref):
    d_inner = d_inner_ref[...]
    even = even_ref[...] > 0

    def step(chip, carry):
        part = contract(d_inner, w_in_ref[chip], 1, 1)
        split_parts(even, part, keep_ref, give_ref, chip)
        return carry

    lax.fori_loop(0, w_in_ref.shape[0], step, 0, unroll=2)


def on_device(
    tokens,
    w_in,
    conv_weight,
    w_dtlow,
    w_bc,
    w_dt,
    dt_bias,
    a_log,
    d_skip,
    w_out,
    cotangent,
    err_in,
    err_out,
):
    tensor = lax.axis_size("tensor")
    replicas = lax.axis_size("dp")
    rows, block = tokens.shape
    chips = tensor // 2
    side = int(replicas**0.5)
    channels = w_in.shape[1]
    width = w_in.shape[0]
    rank = w_dt.shape[0]
    small_width = rank + w_bc.shape[1]
    bf16, f32 = jnp.bfloat16, jnp.float32
    ring = [list(range(core, tensor, 2)) for core in range(2)]
    swap = [(i, i ^ 1) for i in range(tensor)]
    core = lax.rem(lax.axis_index("tensor"), 2)
    even = jnp.full((1, 1), 1 - core, jnp.int32)

    def exchange(parts, axis, groups=None):
        return lax.all_to_all(
            parts, axis, split_axis=0, concat_axis=0, tiled=True, axis_index_groups=groups
        )

    def spread(value, axis, size, groups=None):
        return exchange(jnp.broadcast_to(value[None], (size, *value.shape)), axis, groups)

    def other_core(value):
        return lax.ppermute(value, "tensor", swap)

    inside, left = pl.BlockSpec(memory_space=pltpu.VMEM), pl.BlockSpec(memory_space=pl.ANY)

    def pair_sum(keep, give, *after):
        (total,) = local_call(
            pair_kernel, ((keep.shape, bf16),), specs=[inside, inside] + [left] * len(after)
        )(keep, other_core(give), *after)
        return total

    def sum_channels(chip, *after):
        share = exchange(chip.reshape(chips, rows // chips, chip.shape[1]), "tensor", ring)
        (total,) = local_call(
            share_kernel, ((share.shape, bf16),), specs=[inside] + [left] * len(after)
        )(share, *after)
        return exchange(total, "tensor", ring).reshape(chip.shape)

    def to_owner(array, shift_of, stride):
        place = shift_of(lax.axis_index("dp"))

        def entry(ahead):
            return lax.dynamic_index_in_dim(array, lax.rem(place + ahead, side), 0, False)

        total = entry(0).astype(f32)
        for ahead in range(1, side):
            perm = [
                (i, i + ((shift_of(i) + ahead) % side - shift_of(i)) * stride) for i in range(replicas)
            ]
            total = total + lax.ppermute(entry(ahead), "dp", perm).astype(f32)
        return total

    def along_x(parts):
        return to_owner(parts, lambda i: i // side, side)

    def along_y(parts):
        return to_owner(parts, lambda i: i % side, 1)

    w_in_full = spread(w_in, "dp", replicas)
    w_out_full = lax.all_gather(w_out, "dp", axis=0)
    mine = lax.all_gather(tokens, "tensor", axis=0, axis_index_groups=ring)
    whole, pre, conv_out, small = local_call(
        inner_kernel,
        (
            ((chips, rows, 2 * block), bf16),
            ((rows, channels), f32),
            ((rows, channels), bf16),
            ((rows, small_width), bf16),
        ),
        [pltpu.VMEM((rows, channels), f32)],
    )(mine, other_core(mine), even, w_in_full, conv_weight, w_dtlow, w_bc)
    tiles = pl.cdiv(small_width, block)
    ahead = pl.cdiv(tiles * (rows // chips), 16) * 16
    (packed,) = local_call(pack_kernel, (((chips, ahead + rows, block), bf16),))(
        small, other_core(small), cotangent
    )
    packed = exchange(packed, "tensor", ring)
    (total,) = local_call(
        unpack_kernel,
        (((chips, rows // chips, small_width), bf16),),
        specs=[pl.BlockSpec((chips, ahead, block), lambda step: (0, 0, 0)), left],
    )(packed, w_out_full)
    small = exchange(total, "tensor", ring).reshape(rows, small_width)
    cot_mine = packed[:, ahead:]
    cot_whole, d_hidden = local_call(
        cotangent_kernel,
        (((chips, rows, 2 * block), bf16), ((rows, channels), f32)),
    )(cot_mine, other_core(cot_mine), even, w_out_full)
    hidden_out, d_conv, back = local_call(
        scan_kernel,
        (((rows, channels), bf16), ((rows, channels), f32), ((rows, small_width), bf16)),
        [pltpu.VMEM((rows, channels), f32)] * 5
        + [pltpu.VMEM((rows + 1, a_log.shape[1], channels), f32)],
    )(small, w_dt, dt_bias[None, :], -jnp.exp(a_log).T, d_skip[None, :], conv_out, d_hidden)
    back_chip = pair_sum(back, back)
    (sign_out,) = local_call(sign_out_kernel, (((chips, width, channels), bf16),), specs=[inside, inside, left])(
        hidden_out, cot_whole, back_chip
    )
    out_parts = local_call(
        out_kernel,
        (((chips, rows, block), f32), ((chips, rows, block), bf16)),
        specs=[inside] * 3 + [left],
    )(hidden_out, w_out_full, even, back_chip)
    back = sum_channels(back_chip, sign_out, *out_parts)
    d_inner, sign_in = local_call(
        sign_in_kernel,
        (((rows, channels), bf16), ((side, side, width, channels), bf16)),
    )(back, w_dtlow, w_bc, d_conv, pre, conv_weight, whole)
    votes_in = along_x(along_y(sign_in).astype(bf16))
    votes_out = along_y(along_x(sign_out.reshape(side, side, width, channels)).astype(bf16))
    grad_parts = local_call(
        grad_kernel,
        (((chips, rows, block), f32), ((chips, rows, block), bf16)),
    )(d_inner, w_in_full, even)
    (parts,) = local_call(pairs_kernel, (((chips, 2 * rows, block), bf16),))(
        out_parts[0], other_core(out_parts[1]), grad_parts[0], other_core(grad_parts[1])
    )
    sums = jnp.sum(exchange(parts, "tensor", ring).astype(f32), axis=0).astype(bf16)
    merged_in = votes_in / replicas + err_in
    merged_out = votes_out / replicas + err_out
    update_in = jnp.tanh(4.0 * merged_in)
    update_out = jnp.tanh(4.0 * merged_out)
    return (
        sums[:rows],
        sums[rows:],
        update_in,
        merged_in - update_in,
        update_out,
        merged_out - update_out,
    )


def solution(mesh):
    return jax.shard_map(
        on_device,
        mesh=mesh,
        in_specs=(
            P("dp", "tensor"),
            P("dp", "tensor"),
            P(None, "tensor"),
            P("tensor", None),
            P("tensor", None),
            P(None, "tensor"),
            P("tensor"),
            P("tensor", None),
            P("tensor"),
            P("tensor", "dp"),
            P("dp", "tensor"),
            P("dp", "tensor"),
            P("tensor", "dp"),
        ),
        out_specs=(
            P("dp", "tensor"),
            P("dp", "tensor"),
            P("dp", "tensor"),
            P("dp", "tensor"),
            P("tensor", "dp"),
            P("tensor", "dp"),
        ),
        check_vma=False,
    )
```

```python
import jax
import jax.numpy as jnp
from jax import lax
from jax.experimental import pallas as pl
from jax.experimental.pallas import tpu as pltpu
from jax.sharding import PartitionSpec as P

QB = 128


eps_scale = 1e-06


def contract(left, right, left_dim, right_dim):
    return lax.dot_general(
        left, right, (((left_dim,), (right_dim,)), ((), ())), preferred_element_type=jnp.float32
    )


def identity(size):
    rows = lax.broadcasted_iota(jnp.int32, (size, size), 0)
    cols = lax.broadcasted_iota(jnp.int32, (size, size), 1)
    return jnp.where(rows == cols, 1.0, 0.0).astype(jnp.bfloat16)


def scan_kernel(
    small_ref, w_dt_ref, bias_ref, a_neg_ref, skip_ref, conv_ref, dh_ref,
    hidden_ref, dconv_ref, back_ref,
    delta_s, x_s, u_s, y_s, dd_s, states,
):
    tokens, channels = conv_ref.shape
    n = a_neg_ref.shape[0]
    rank = w_dt_ref.shape[0]
    low = small_ref[:, :rank]
    pre = jnp.dot(low, w_dt_ref[...], preferred_element_type=jnp.float32) + bias_ref[...]
    delta = jax.nn.softplus(pre)
    x = conv_ref[...].astype(jnp.float32)
    delta_s[...] = delta
    x_s[...] = x
    u_s[...] = delta * x
    maps = contract(identity(2 * n), small_ref[:, rank:], 1, 1)
    a_neg = a_neg_ref[...]
    skip = skip_ref[...]
    states[0] = jnp.zeros((n, channels), jnp.float32)

    def columns(rolled, row, j):
        return jnp.broadcast_to(rolled[row : row + n, j : j + 1], (n, channels))

    def forward(chunk, h):
        start = pl.multiple_of(chunk * 8, 8)
        d8 = delta_s[pl.ds(start, 8), :]
        x8 = x_s[pl.ds(start, 8), :]
        u8 = u_s[pl.ds(start, 8), :]
        rolled = pltpu.roll(maps, lax.rem(tokens - start, tokens), 1)
        rows = []
        for j in range(8):
            h = jnp.exp(d8[j : j + 1] * a_neg) * h + u8[j : j + 1] * columns(rolled, 0, j)
            states[start + j + 1] = h
            rows.append(jnp.sum(h * columns(rolled, n, j), axis=0, keepdims=True))
        y_s[pl.ds(start, 8), :] = jnp.concatenate(rows, axis=0) + skip * x8
        return h

    lax.fori_loop(0, tokens // 8, forward, jnp.zeros((n, channels), jnp.float32))
    hidden_ref[...] = y_s[...].astype(hidden_ref.dtype)
    lane = lax.broadcasted_iota(jnp.int32, (n, tokens), 1)

    def backward(step, carry):
        g_next, acc_b, acc_c = carry
        start = pl.multiple_of(tokens - 8 - step * 8, 8)
        d8 = delta_s[pl.ds(start, 8), :]
        x8 = x_s[pl.ds(start, 8), :]
        u8 = u_s[pl.ds(start, 8), :]
        dy8 = dh_ref[pl.ds(start, 8), :]
        rolled = pltpu.roll(maps, lax.rem(tokens - start, tokens), 1)
        rows_a, rows_b = [None] * 8, [None] * 8
        for j in range(7, -1, -1):
            dy = dy8[j : j + 1]
            g = g_next + dy * columns(rolled, n, j)
            here = lane == start + j
            acc_c = jnp.where(here, jnp.sum(dy * states[start + j + 1], axis=1, keepdims=True), acc_c)
            acc_b = jnp.where(here, jnp.sum(g * u8[j : j + 1], axis=1, keepdims=True), acc_b)
            rows_b[j] = jnp.sum(g * columns(rolled, 0, j), axis=0, keepdims=True)
            g_next = g * jnp.exp(d8[j : j + 1] * a_neg)
            rows_a[j] = jnp.sum(g_next * (states[start + j] * a_neg), axis=0, keepdims=True)
        sum_b = jnp.concatenate(rows_b, axis=0)
        dd_s[pl.ds(start, 8), :] = jnp.concatenate(rows_a, axis=0) + x8 * sum_b
        dconv_ref[pl.ds(start, 8), :] = d8 * sum_b + skip * dy8
        return g_next, acc_b, acc_c

    zero = jnp.zeros((n, tokens), jnp.float32)
    _, acc_b, acc_c = lax.fori_loop(
        0, tokens // 8, backward, (jnp.zeros((n, channels), jnp.float32), zero, zero)
    )
    d_pre = (dd_s[...] * jax.nn.sigmoid(pre)).astype(jnp.bfloat16)
    back_ref[:, :rank] = contract(d_pre, w_dt_ref[...], 1, 1).astype(back_ref.dtype)
    both = jnp.concatenate([acc_b, acc_c], axis=0).astype(jnp.bfloat16)
    back_ref[:, rank:] = contract(identity(tokens), both, 1, 1).astype(back_ref.dtype)


VMEM_BYTES = 16 << 20


def local_call(kernel, shapes, scratch=(), specs=None):
    more = {} if specs is None else {"grid": (1,), "in_specs": specs}
    return pl.pallas_call(
        kernel,
        **more,
        out_shape=tuple(jax.ShapeDtypeStruct(shape, kind) for shape, kind in shapes),
        scratch_shapes=list(scratch),
        compiler_params=pltpu.CompilerParams(vmem_limit_bytes=VMEM_BYTES),
    )


def pair_kernel(keep_ref, give_ref, *refs):
    refs[-1][...] = (keep_ref[...].astype(jnp.float32) + give_ref[...].astype(jnp.float32)).astype(jnp.bfloat16)


def pairs_kernel(keep_out_ref, give_out_ref, keep_in_ref, give_in_ref, after_ref, total_ref):
    rows = keep_out_ref.shape[1]
    out = keep_out_ref[...] + give_out_ref[...].astype(jnp.float32)
    total_ref[:, :rows, :] = out.astype(jnp.bfloat16)
    grad = keep_in_ref[...] + give_in_ref[...].astype(jnp.float32)
    total_ref[:, rows:, :] = grad.astype(jnp.bfloat16)


def share_kernel(parts_ref, *refs):
    total = jnp.sum(parts_ref[...].astype(jnp.float32), axis=0).astype(jnp.bfloat16)
    refs[-1][...] = jnp.broadcast_to(total[None], parts_ref.shape)


def pack_kernel(mine_ref, other_ref, block_ref, packed_ref):
    chips, height, lanes = packed_ref.shape
    rows, width = mine_ref.shape
    ahead = height - rows
    total = mine_ref[...].astype(jnp.float32) + other_ref[...].astype(jnp.float32)
    tiles = pl.cdiv(width, lanes)
    total = jnp.concatenate([total, jnp.zeros((rows, tiles * lanes - width), jnp.float32)], axis=1)
    share = total.reshape(chips, rows // chips, tiles * lanes)
    pieces = [share[:, :, i * lanes : (i + 1) * lanes] for i in range(tiles)]
    spare = ahead - tiles * (rows // chips)
    if spare:
        pieces.append(jnp.zeros((chips, spare, lanes), jnp.float32))
    packed_ref[:, :ahead, :] = jnp.concatenate(pieces, axis=1).astype(jnp.bfloat16)
    packed_ref[:, ahead:, :] = jnp.broadcast_to(block_ref[...][None], (chips, rows, lanes))


def unpack_kernel(parts_ref, after_ref, total_ref):
    _, height, width = total_ref.shape
    lanes = parts_ref.shape[2]
    total = jnp.sum(parts_ref[...].astype(jnp.float32), axis=0)
    pieces = [total[i * height : (i + 1) * height] for i in range(pl.cdiv(width, lanes))]
    total = jnp.concatenate(pieces, axis=1)[:, :width].astype(jnp.bfloat16)
    total_ref[...] = jnp.broadcast_to(total[None], total_ref.shape)


def in_order(even, mine, other):
    return jnp.concatenate([jnp.where(even, mine, other), jnp.where(even, other, mine)], axis=1)


def inner_kernel(
    mine_ref, other_ref, even_ref, w_in_ref, taps_ref, low_ref, bc_ref,
    whole_ref, pre_ref, conv_ref, small_ref, total_s,
):
    chips, rows, block = mine_ref.shape
    even = even_ref[...] > 0

    def step(chip, carry):
        features = in_order(even, mine_ref[chip], other_ref[chip])
        whole_ref[chip] = features
        total_s[...] += jnp.dot(features, w_in_ref[chip], preferred_element_type=jnp.float32)
        return carry

    total_s[...] = jnp.zeros_like(total_s)
    lax.fori_loop(0, chips, step, 0, unroll=4)
    inner = total_s[...].astype(jnp.bfloat16).astype(jnp.float32)
    taps = taps_ref[...]
    width = taps.shape[0]
    row = lax.broadcasted_iota(jnp.int32, inner.shape, 0)
    pre = taps[width - 1 :] * inner
    for back in range(1, width):
        shifted = jnp.where(row >= back, pltpu.roll(inner, back, 0), 0.0)
        pre = pre + taps[width - 1 - back : width - back] * shifted
    conv = (pre / (1.0 + jnp.exp(-pre))).astype(jnp.bfloat16)
    pre_ref[...] = pre
    conv_ref[...] = conv
    rank = low_ref.shape[1]
    small_ref[:, :rank] = jnp.dot(conv, low_ref[...], preferred_element_type=jnp.float32).astype(jnp.bfloat16)
    small_ref[:, rank:] = jnp.dot(conv, bc_ref[...], preferred_element_type=jnp.float32).astype(jnp.bfloat16)


def cotangent_kernel(mine_ref, other_ref, even_ref, w_out_ref, whole_ref, hidden_ref):
    chips = w_out_ref.shape[0]
    even = even_ref[...] > 0

    def step(chip, carry):
        features = in_order(even, mine_ref[chip], other_ref[chip])
        whole_ref[chip] = features
        hidden_ref[...] += contract(features, w_out_ref[chip], 1, 1)
        return carry

    hidden_ref[...] = jnp.zeros_like(hidden_ref)
    lax.fori_loop(0, chips, step, 0, unroll=4)


def coded(part):
    scale = (jnp.max(jnp.abs(part), axis=1, keepdims=True) + eps_scale).astype(jnp.bfloat16)
    scale = scale.astype(jnp.float32)
    return (part / scale).astype(jnp.bfloat16).astype(jnp.float32) * scale


def split_parts(even, part, keep_ref, give_ref, chip):
    first, second = coded(part[:, :QB]), coded(part[:, QB:])
    keep_ref[chip] = jnp.where(even, first, second)
    give_ref[chip] = jnp.where(even, second, first).astype(give_ref.dtype)


def soft_sign(grad):
    signs = []
    for start in range(0, grad.shape[1], QB):
        part = grad[:, start : start + QB]
        mean = jnp.mean(jnp.abs(part), axis=1, keepdims=True) + eps_scale
        signs.append(jnp.tanh(part / mean).astype(jnp.bfloat16))
    return jnp.concatenate(signs, axis=1)


def sign_out_kernel(hidden_ref, cot_ref, after_ref, sign_ref):
    hidden = hidden_ref[...]

    def step(chip, carry):
        sign_ref[chip] = soft_sign(contract(hidden, cot_ref[chip], 0, 0))
        return carry

    lax.fori_loop(0, cot_ref.shape[0], step, 0, unroll=2)


def out_kernel(hidden_ref, w_out_ref, even_ref, after_ref, keep_ref, give_ref):
    hidden = hidden_ref[...]
    even = even_ref[...] > 0

    def step(chip, carry):
        part = jnp.dot(hidden, w_out_ref[chip], preferred_element_type=jnp.float32)
        split_parts(even, part, keep_ref, give_ref, chip)
        return carry

    lax.fori_loop(0, w_out_ref.shape[0], step, 0, unroll=2)


def grad_kernel(
    back_ref, low_ref, bc_ref, d_conv_ref, pre_ref, taps_ref, w_in_ref, even_ref, *refs
):
    d_inner_ref, keep_ref, give_ref = refs[-3:]
    rank = low_ref.shape[1]
    back = back_ref[...]
    d_conv = (
        d_conv_ref[...]
        + contract(back[:, :rank], low_ref[...], 1, 1)
        + contract(back[:, rank:], bc_ref[...], 1, 1)
    )
    pre = pre_ref[...]
    gate = jax.nn.sigmoid(pre)
    d_sum = d_conv * (gate * (1.0 + pre * (1.0 - gate)))
    taps = taps_ref[...]
    width = taps.shape[0]
    rows = d_sum.shape[0]
    row = lax.broadcasted_iota(jnp.int32, d_sum.shape, 0)
    d_inner = taps[width - 1 :] * d_sum
    for ahead in range(1, width):
        shifted = jnp.where(row < rows - ahead, pltpu.roll(d_sum, rows - ahead, 0), 0.0)
        d_inner = d_inner + taps[width - 1 - ahead : width - ahead] * shifted
    d_inner = d_inner.astype(jnp.bfloat16)
    d_inner_ref[...] = d_inner

    even = even_ref[...] > 0

    def step(chip, carry):
        part = contract(d_inner, w_in_ref[chip], 1, 1)
        split_parts(even, part, keep_ref, give_ref, chip)
        return carry

    lax.fori_loop(0, w_in_ref.shape[0], step, 0, unroll=2)


def sign_in_kernel(d_inner_ref, whole_ref, sign_ref):
    d_inner = d_inner_ref[...]
    side = sign_ref.shape[0]

    def step(chip, carry):
        sign = soft_sign(contract(whole_ref[chip], d_inner, 0, 0))
        sign_ref[lax.rem(chip, side), lax.div(chip, side)] = sign
        return carry

    lax.fori_loop(0, whole_ref.shape[0], step, 0, unroll=2)


def on_device(
    tokens,
    w_in,
    conv_weight,
    w_dtlow,
    w_bc,
    w_dt,
    dt_bias,
    a_log,
    d_skip,
    w_out,
    cotangent,
    err_in,
    err_out,
):
    tensor = lax.axis_size("tensor")
    replicas = lax.axis_size("dp")
    rows, block = tokens.shape
    chips = tensor // 2
    side = int(replicas**0.5)
    channels = w_in.shape[1]
    width = w_in.shape[0]
    rank = w_dt.shape[0]
    small_width = rank + w_bc.shape[1]
    bf16, f32 = jnp.bfloat16, jnp.float32
    ring = [list(range(core, tensor, 2)) for core in range(2)]
    swap = [(i, i ^ 1) for i in range(tensor)]
    core = lax.rem(lax.axis_index("tensor"), 2)
    even = jnp.full((1, 1), 1 - core, jnp.int32)

    def exchange(parts, axis, groups=None):
        return lax.all_to_all(
            parts, axis, split_axis=0, concat_axis=0, tiled=True, axis_index_groups=groups
        )

    def spread(value, axis, size, groups=None):
        return exchange(jnp.broadcast_to(value[None], (size, *value.shape)), axis, groups)

    def other_core(value):
        return lax.ppermute(value, "tensor", swap)

    inside, left = pl.BlockSpec(memory_space=pltpu.VMEM), pl.BlockSpec(memory_space=pl.ANY)

    def pair_sum(keep, give, *after):
        (total,) = local_call(
            pair_kernel, ((keep.shape, bf16),), specs=[inside, inside] + [left] * len(after)
        )(keep, other_core(give), *after)
        return total

    def sum_shares(chip, *after):
        share = exchange(chip.reshape(chips, rows // chips, chip.shape[1]), "tensor", ring)
        (total,) = local_call(
            share_kernel, ((share.shape, bf16),), specs=[inside] + [left] * len(after)
        )(share, *after)
        return total

    def sum_channels(chip, *after):
        return exchange(sum_shares(chip, *after), "tensor", ring).reshape(chip.shape)

    def to_owner(array, shift_of, stride):
        place = shift_of(lax.axis_index("dp"))

        def entry(ahead):
            return lax.dynamic_index_in_dim(array, lax.rem(place + ahead, side), 0, False)

        total = entry(0).astype(f32)
        for ahead in range(1, side):
            perm = [
                (i, i + ((shift_of(i) + ahead) % side - shift_of(i)) * stride) for i in range(replicas)
            ]
            total = total + lax.ppermute(entry(ahead), "dp", perm).astype(f32)
        return total

    def along_x(parts):
        return to_owner(parts, lambda i: i // side, side)

    def along_y(parts):
        return to_owner(parts, lambda i: i % side, 1)

    w_in_full = spread(w_in, "dp", replicas)
    w_out_full = lax.all_gather(w_out, "dp", axis=0)
    mine = lax.all_gather(tokens, "tensor", axis=0, axis_index_groups=ring)
    whole, pre, conv_out, small = local_call(
        inner_kernel,
        (
            ((chips, rows, 2 * block), bf16),
            ((rows, channels), f32),
            ((rows, channels), bf16),
            ((rows, small_width), bf16),
        ),
        [pltpu.VMEM((rows, channels), f32)],
    )(mine, other_core(mine), even, w_in_full, conv_weight, w_dtlow, w_bc)
    tiles = pl.cdiv(small_width, block)
    ahead = pl.cdiv(tiles * (rows // chips), 16) * 16
    (packed,) = local_call(pack_kernel, (((chips, ahead + rows, block), bf16),))(
        small, other_core(small), cotangent
    )
    packed = exchange(packed, "tensor", ring)
    (total,) = local_call(
        unpack_kernel,
        (((chips, rows // chips, small_width), bf16),),
        specs=[pl.BlockSpec((chips, ahead, block), lambda step: (0, 0, 0)), left],
    )(packed, w_out_full)
    small = exchange(total, "tensor", ring).reshape(rows, small_width)
    cot_mine = packed[:, ahead:]
    cot_whole, d_hidden = local_call(
        cotangent_kernel,
        (((chips, rows, 2 * block), bf16), ((rows, channels), f32)),
    )(cot_mine, other_core(cot_mine), even, w_out_full)
    hidden_out, d_conv, back = local_call(
        scan_kernel,
        (((rows, channels), bf16), ((rows, channels), f32), ((rows, small_width), bf16)),
        [pltpu.VMEM((rows, channels), f32)] * 5
        + [pltpu.VMEM((rows + 1, a_log.shape[1], channels), f32)],
    )(small, w_dt, dt_bias[None, :], -jnp.exp(a_log).T, d_skip[None, :], conv_out, d_hidden)
    back_chip = pair_sum(back, back)
    (sign_out,) = local_call(
        sign_out_kernel, (((chips, width, channels), bf16),), specs=[inside, inside, left]
    )(hidden_out, cot_whole, back_chip)
    votes_out = along_x(sign_out.reshape(side, side, width, channels)).astype(bf16)
    total = sum_shares(back_chip, sign_out)
    out_parts = local_call(
        out_kernel,
        (((chips, rows, block), f32), ((chips, rows, block), bf16)),
        specs=[inside] * 3 + [left],
    )(hidden_out, w_out_full, even, total)
    back = exchange(total, "tensor", ring).reshape(back_chip.shape)
    d_inner, *grad_parts = local_call(
        grad_kernel,
        (
            ((rows, channels), bf16),
            ((chips, rows, block), f32),
            ((chips, rows, block), bf16),
        ),
        specs=[inside] * 8 + [left] * 2,
    )(back, w_dtlow, w_bc, d_conv, pre, conv_weight, w_in_full, even, votes_out, out_parts[0])
    (sign_in,) = local_call(
        sign_in_kernel, (((side, side, width, channels), bf16),), specs=[inside, inside]
    )(d_inner, whole)
    votes_in = along_x(along_y(sign_in).astype(bf16))
    votes_out = along_y(votes_out)
    (parts,) = local_call(
        pairs_kernel, (((chips, 2 * rows, block), bf16),), specs=[inside] * 4 + [left]
    )(out_parts[0], other_core(out_parts[1]), grad_parts[0], other_core(grad_parts[1]), sign_in)
    sums = jnp.sum(exchange(parts, "tensor", ring).astype(f32), axis=0).astype(bf16)
    merged_in = votes_in / replicas + err_in
    merged_out = votes_out / replicas + err_out
    update_in = jnp.tanh(4.0 * merged_in)
    update_out = jnp.tanh(4.0 * merged_out)
    return (
        sums[:rows],
        sums[rows:],
        update_in,
        merged_in - update_in,
        update_out,
        merged_out - update_out,
    )


def solution(mesh):
    return jax.shard_map(
        on_device,
        mesh=mesh,
        in_specs=(
            P("dp", "tensor"),
            P("dp", "tensor"),
            P(None, "tensor"),
            P("tensor", None),
            P("tensor", None),
            P(None, "tensor"),
            P("tensor"),
            P("tensor", None),
            P("tensor"),
            P("tensor", "dp"),
            P("dp", "tensor"),
            P("dp", "tensor"),
            P("tensor", "dp"),
        ),
        out_specs=(
            P("dp", "tensor"),
            P("dp", "tensor"),
            P("dp", "tensor"),
            P("dp", "tensor"),
            P("tensor", "dp"),
            P("tensor", "dp"),
        ),
        check_vma=False,
    )
```

```python
import jax
import jax.numpy as jnp
from jax import lax
from jax.experimental import pallas as pl
from jax.experimental.pallas import tpu as pltpu
from jax.sharding import PartitionSpec as P

QB = 128


eps_scale = 1e-06


def contract(left, right, left_dim, right_dim):
    return lax.dot_general(
        left, right, (((left_dim,), (right_dim,)), ((), ())), preferred_element_type=jnp.float32
    )


def identity(size):
    rows = lax.broadcasted_iota(jnp.int32, (size, size), 0)
    cols = lax.broadcasted_iota(jnp.int32, (size, size), 1)
    return jnp.where(rows == cols, 1.0, 0.0).astype(jnp.bfloat16)


def scan_kernel(
    small_ref, w_dt_ref, bias_ref, a_neg_ref, skip_ref, conv_ref, dh_ref,
    hidden_ref, dconv_ref, back_ref,
    delta_s, x_s, u_s, y_s, dd_s, states,
):
    tokens, channels = conv_ref.shape
    n = a_neg_ref.shape[0]
    rank = w_dt_ref.shape[0]
    low = small_ref[:, :rank]
    pre = jnp.dot(low, w_dt_ref[...], preferred_element_type=jnp.float32) + bias_ref[...]
    delta = jax.nn.softplus(pre)
    x = conv_ref[...].astype(jnp.float32)
    delta_s[...] = delta
    x_s[...] = x
    u_s[...] = delta * x
    maps = contract(identity(2 * n), small_ref[:, rank:], 1, 1)
    a_neg = a_neg_ref[...]
    skip = skip_ref[...]
    states[0] = jnp.zeros((n, channels), jnp.float32)

    def columns(rolled, row, j):
        return jnp.broadcast_to(rolled[row : row + n, j : j + 1], (n, channels))

    def forward(chunk, h):
        start = pl.multiple_of(chunk * 8, 8)
        d8 = delta_s[pl.ds(start, 8), :]
        x8 = x_s[pl.ds(start, 8), :]
        u8 = u_s[pl.ds(start, 8), :]
        rolled = pltpu.roll(maps, lax.rem(tokens - start, tokens), 1)
        rows = []
        for j in range(8):
            h = jnp.exp(d8[j : j + 1] * a_neg) * h + u8[j : j + 1] * columns(rolled, 0, j)
            states[start + j + 1] = h
            rows.append(jnp.sum(h * columns(rolled, n, j), axis=0, keepdims=True))
        y_s[pl.ds(start, 8), :] = jnp.concatenate(rows, axis=0) + skip * x8
        return h

    lax.fori_loop(0, tokens // 8, forward, jnp.zeros((n, channels), jnp.float32))
    hidden_ref[...] = y_s[...].astype(hidden_ref.dtype)
    lane = lax.broadcasted_iota(jnp.int32, (n, tokens), 1)

    def backward(step, carry):
        g_next, acc_b, acc_c = carry
        start = pl.multiple_of(tokens - 8 - step * 8, 8)
        d8 = delta_s[pl.ds(start, 8), :]
        x8 = x_s[pl.ds(start, 8), :]
        u8 = u_s[pl.ds(start, 8), :]
        dy8 = dh_ref[pl.ds(start, 8), :]
        rolled = pltpu.roll(maps, lax.rem(tokens - start, tokens), 1)
        rows_a, rows_b = [None] * 8, [None] * 8
        for j in range(7, -1, -1):
            dy = dy8[j : j + 1]
            g = g_next + dy * columns(rolled, n, j)
            here = lane == start + j
            acc_c = jnp.where(here, jnp.sum(dy * states[start + j + 1], axis=1, keepdims=True), acc_c)
            acc_b = jnp.where(here, jnp.sum(g * u8[j : j + 1], axis=1, keepdims=True), acc_b)
            rows_b[j] = jnp.sum(g * columns(rolled, 0, j), axis=0, keepdims=True)
            g_next = g * jnp.exp(d8[j : j + 1] * a_neg)
            rows_a[j] = jnp.sum(g_next * (states[start + j] * a_neg), axis=0, keepdims=True)
        sum_b = jnp.concatenate(rows_b, axis=0)
        dd_s[pl.ds(start, 8), :] = jnp.concatenate(rows_a, axis=0) + x8 * sum_b
        dconv_ref[pl.ds(start, 8), :] = d8 * sum_b + skip * dy8
        return g_next, acc_b, acc_c

    zero = jnp.zeros((n, tokens), jnp.float32)
    _, acc_b, acc_c = lax.fori_loop(
        0, tokens // 8, backward, (jnp.zeros((n, channels), jnp.float32), zero, zero)
    )
    d_pre = (dd_s[...] * jax.nn.sigmoid(pre)).astype(jnp.bfloat16)
    back_ref[:, :rank] = contract(d_pre, w_dt_ref[...], 1, 1).astype(back_ref.dtype)
    both = jnp.concatenate([acc_b, acc_c], axis=0).astype(jnp.bfloat16)
    back_ref[:, rank:] = contract(identity(tokens), both, 1, 1).astype(back_ref.dtype)


VMEM_BYTES = 16 << 20


def local_call(kernel, shapes, scratch=(), specs=None):
    more = {} if specs is None else {"grid": (1,), "in_specs": specs}
    return pl.pallas_call(
        kernel,
        **more,
        out_shape=tuple(jax.ShapeDtypeStruct(shape, kind) for shape, kind in shapes),
        scratch_shapes=list(scratch),
        compiler_params=pltpu.CompilerParams(vmem_limit_bytes=VMEM_BYTES),
    )


def pair_kernel(keep_ref, give_ref, *refs):
    refs[-1][...] = (keep_ref[...].astype(jnp.float32) + give_ref[...].astype(jnp.float32)).astype(jnp.bfloat16)


def pairs_kernel(keep_out_ref, give_out_ref, keep_in_ref, give_in_ref, after_ref, total_ref):
    rows = keep_out_ref.shape[1]
    out = keep_out_ref[...] + give_out_ref[...].astype(jnp.float32)
    total_ref[:, :rows, :] = out.astype(jnp.bfloat16)
    grad = keep_in_ref[...] + give_in_ref[...].astype(jnp.float32)
    total_ref[:, rows:, :] = grad.astype(jnp.bfloat16)


def share_kernel(parts_ref, *refs):
    total = jnp.sum(parts_ref[...].astype(jnp.float32), axis=0).astype(jnp.bfloat16)
    refs[-1][...] = jnp.broadcast_to(total[None], parts_ref.shape)


def pack_kernel(mine_ref, other_ref, block_ref, packed_ref):
    chips, height, lanes = packed_ref.shape
    rows, width = mine_ref.shape
    ahead = height - rows
    total = mine_ref[...].astype(jnp.float32) + other_ref[...].astype(jnp.float32)
    tiles = pl.cdiv(width, lanes)
    total = jnp.concatenate([total, jnp.zeros((rows, tiles * lanes - width), jnp.float32)], axis=1)
    share = total.reshape(chips, rows // chips, tiles * lanes)
    pieces = [share[:, :, i * lanes : (i + 1) * lanes] for i in range(tiles)]
    spare = ahead - tiles * (rows // chips)
    if spare:
        pieces.append(jnp.zeros((chips, spare, lanes), jnp.float32))
    packed_ref[:, :ahead, :] = jnp.concatenate(pieces, axis=1).astype(jnp.bfloat16)
    packed_ref[:, ahead:, :] = jnp.broadcast_to(block_ref[...][None], (chips, rows, lanes))


def unpack_kernel(parts_ref, after_ref, total_ref):
    _, height, width = total_ref.shape
    lanes = parts_ref.shape[2]
    total = jnp.sum(parts_ref[...].astype(jnp.float32), axis=0)
    pieces = [total[i * height : (i + 1) * height] for i in range(pl.cdiv(width, lanes))]
    total = jnp.concatenate(pieces, axis=1)[:, :width].astype(jnp.bfloat16)
    total_ref[...] = jnp.broadcast_to(total[None], total_ref.shape)


def in_order(even, mine, other):
    return jnp.concatenate([jnp.where(even, mine, other), jnp.where(even, other, mine)], axis=1)


def inner_kernel(
    mine_ref, other_ref, even_ref, w_in_ref, taps_ref, low_ref, bc_ref,
    whole_ref, pre_ref, conv_ref, small_ref, total_s,
):
    chips, rows, block = mine_ref.shape
    even = even_ref[...] > 0

    def step(chip, carry):
        features = in_order(even, mine_ref[chip], other_ref[chip])
        whole_ref[chip] = features
        total_s[...] += jnp.dot(features, w_in_ref[chip], preferred_element_type=jnp.float32)
        return carry

    total_s[...] = jnp.zeros_like(total_s)
    lax.fori_loop(0, chips, step, 0, unroll=4)
    inner = total_s[...].astype(jnp.bfloat16).astype(jnp.float32)
    taps = taps_ref[...]
    width = taps.shape[0]
    row = lax.broadcasted_iota(jnp.int32, inner.shape, 0)
    pre = taps[width - 1 :] * inner
    for back in range(1, width):
        shifted = jnp.where(row >= back, pltpu.roll(inner, back, 0), 0.0)
        pre = pre + taps[width - 1 - back : width - back] * shifted
    conv = (pre / (1.0 + jnp.exp(-pre))).astype(jnp.bfloat16)
    pre_ref[...] = pre
    conv_ref[...] = conv
    rank = low_ref.shape[1]
    small_ref[:, :rank] = jnp.dot(conv, low_ref[...], preferred_element_type=jnp.float32).astype(jnp.bfloat16)
    small_ref[:, rank:] = jnp.dot(conv, bc_ref[...], preferred_element_type=jnp.float32).astype(jnp.bfloat16)


def cotangent_kernel(mine_ref, other_ref, even_ref, w_out_ref, whole_ref, hidden_ref):
    chips = w_out_ref.shape[0]
    even = even_ref[...] > 0

    def step(chip, carry):
        features = in_order(even, mine_ref[chip], other_ref[chip])
        whole_ref[chip] = features
        hidden_ref[...] += contract(features, w_out_ref[chip], 1, 1)
        return carry

    hidden_ref[...] = jnp.zeros_like(hidden_ref)
    lax.fori_loop(0, chips, step, 0, unroll=4)


def coded(part):
    scale = (jnp.max(jnp.abs(part), axis=1, keepdims=True) + eps_scale).astype(jnp.bfloat16)
    scale = scale.astype(jnp.float32)
    return (part / scale).astype(jnp.bfloat16).astype(jnp.float32) * scale


def split_parts(even, part, keep_ref, give_ref, chip):
    first, second = coded(part[:, :QB]), coded(part[:, QB:])
    keep_ref[chip] = jnp.where(even, first, second)
    give_ref[chip] = jnp.where(even, second, first).astype(give_ref.dtype)


def soft_sign(grad):
    signs = []
    for start in range(0, grad.shape[1], QB):
        part = grad[:, start : start + QB]
        mean = jnp.mean(jnp.abs(part), axis=1, keepdims=True) + eps_scale
        signs.append(jnp.tanh(part / mean).astype(jnp.bfloat16))
    return jnp.concatenate(signs, axis=1)


def sign_out_kernel(hidden_ref, cot_ref, after_ref, sign_ref):
    hidden = hidden_ref[...]

    def step(chip, carry):
        sign_ref[chip] = soft_sign(contract(hidden, cot_ref[chip], 0, 0))
        return carry

    lax.fori_loop(0, cot_ref.shape[0], step, 0, unroll=2)


def out_kernel(hidden_ref, w_out_ref, even_ref, after_ref, keep_ref, give_ref):
    hidden = hidden_ref[...]
    even = even_ref[...] > 0

    def step(chip, carry):
        part = jnp.dot(hidden, w_out_ref[chip], preferred_element_type=jnp.float32)
        split_parts(even, part, keep_ref, give_ref, chip)
        return carry

    lax.fori_loop(0, w_out_ref.shape[0], step, 0, unroll=2)


def grad_kernel(
    back_ref, low_ref, bc_ref, d_conv_ref, pre_ref, taps_ref, w_in_ref, even_ref, *refs
):
    d_inner_ref, keep_ref, give_ref = refs[-3:]
    rank = low_ref.shape[1]
    back = back_ref[...]
    d_conv = (
        d_conv_ref[...]
        + contract(back[:, :rank], low_ref[...], 1, 1)
        + contract(back[:, rank:], bc_ref[...], 1, 1)
    )
    pre = pre_ref[...]
    gate = jax.nn.sigmoid(pre)
    d_sum = d_conv * (gate * (1.0 + pre * (1.0 - gate)))
    taps = taps_ref[...]
    width = taps.shape[0]
    rows = d_sum.shape[0]
    row = lax.broadcasted_iota(jnp.int32, d_sum.shape, 0)
    d_inner = taps[width - 1 :] * d_sum
    for ahead in range(1, width):
        shifted = jnp.where(row < rows - ahead, pltpu.roll(d_sum, rows - ahead, 0), 0.0)
        d_inner = d_inner + taps[width - 1 - ahead : width - ahead] * shifted
    d_inner = d_inner.astype(jnp.bfloat16)
    d_inner_ref[...] = d_inner

    even = even_ref[...] > 0

    def step(chip, carry):
        part = contract(d_inner, w_in_ref[chip], 1, 1)
        split_parts(even, part, keep_ref, give_ref, chip)
        return carry

    lax.fori_loop(0, w_in_ref.shape[0], step, 0, unroll=2)


def sign_in_kernel(d_inner_ref, whole_ref, sign_ref):
    d_inner = d_inner_ref[...]
    side = sign_ref.shape[0]

    def step(chip, carry):
        sign = soft_sign(contract(whole_ref[chip], d_inner, 0, 0))
        sign_ref[lax.div(chip, side), lax.rem(chip, side)] = sign
        return carry

    lax.fori_loop(0, whole_ref.shape[0], step, 0, unroll=2)


def on_device(
    tokens,
    w_in,
    conv_weight,
    w_dtlow,
    w_bc,
    w_dt,
    dt_bias,
    a_log,
    d_skip,
    w_out,
    cotangent,
    err_in,
    err_out,
):
    tensor = lax.axis_size("tensor")
    replicas = lax.axis_size("dp")
    rows, block = tokens.shape
    chips = tensor // 2
    side = int(replicas**0.5)
    channels = w_in.shape[1]
    width = w_in.shape[0]
    rank = w_dt.shape[0]
    small_width = rank + w_bc.shape[1]
    bf16, f32 = jnp.bfloat16, jnp.float32
    ring = [list(range(core, tensor, 2)) for core in range(2)]
    swap = [(i, i ^ 1) for i in range(tensor)]
    core = lax.rem(lax.axis_index("tensor"), 2)
    even = jnp.full((1, 1), 1 - core, jnp.int32)

    def exchange(parts, axis, groups=None):
        return lax.all_to_all(
            parts, axis, split_axis=0, concat_axis=0, tiled=True, axis_index_groups=groups
        )

    def spread(value, axis, size, groups=None):
        return exchange(jnp.broadcast_to(value[None], (size, *value.shape)), axis, groups)

    def other_core(value):
        return lax.ppermute(value, "tensor", swap)

    inside, left = pl.BlockSpec(memory_space=pltpu.VMEM), pl.BlockSpec(memory_space=pl.ANY)

    def pair_sum(keep, give, *after):
        (total,) = local_call(
            pair_kernel, ((keep.shape, bf16),), specs=[inside, inside] + [left] * len(after)
        )(keep, other_core(give), *after)
        return total

    def sum_shares(chip, *after):
        share = exchange(chip.reshape(chips, rows // chips, chip.shape[1]), "tensor", ring)
        (total,) = local_call(
            share_kernel, ((share.shape, bf16),), specs=[inside] + [left] * len(after)
        )(share, *after)
        return total

    def sum_channels(chip, *after):
        return exchange(sum_shares(chip, *after), "tensor", ring).reshape(chip.shape)

    def to_owner(array, shift_of, stride):
        place = shift_of(lax.axis_index("dp"))

        def entry(ahead):
            return lax.dynamic_index_in_dim(array, lax.rem(place + ahead, side), 0, False)

        total = entry(0).astype(f32)
        for ahead in range(1, side):
            perm = [
                (i, i + ((shift_of(i) + ahead) % side - shift_of(i)) * stride) for i in range(replicas)
            ]
            total = total + lax.ppermute(entry(ahead), "dp", perm).astype(f32)
        return total

    def along_x(parts):
        return to_owner(parts, lambda i: i // side, side)

    def along_y(parts):
        return to_owner(parts, lambda i: i % side, 1)

    w_in_full = spread(w_in, "dp", replicas)
    w_out_full = lax.all_gather(w_out, "dp", axis=0)
    mine = lax.all_gather(tokens, "tensor", axis=0, axis_index_groups=ring)
    whole, pre, conv_out, small = local_call(
        inner_kernel,
        (
            ((chips, rows, 2 * block), bf16),
            ((rows, channels), f32),
            ((rows, channels), bf16),
            ((rows, small_width), bf16),
        ),
        [pltpu.VMEM((rows, channels), f32)],
    )(mine, other_core(mine), even, w_in_full, conv_weight, w_dtlow, w_bc)
    tiles = pl.cdiv(small_width, block)
    ahead = pl.cdiv(tiles * (rows // chips), 16) * 16
    (packed,) = local_call(pack_kernel, (((chips, ahead + rows, block), bf16),))(
        small, other_core(small), cotangent
    )
    packed = exchange(packed, "tensor", ring)
    (total,) = local_call(
        unpack_kernel,
        (((chips, rows // chips, small_width), bf16),),
        specs=[pl.BlockSpec((chips, ahead, block), lambda step: (0, 0, 0)), left],
    )(packed, w_out_full)
    small = exchange(total, "tensor", ring).reshape(rows, small_width)
    cot_mine = packed[:, ahead:]
    cot_whole, d_hidden = local_call(
        cotangent_kernel,
        (((chips, rows, 2 * block), bf16), ((rows, channels), f32)),
    )(cot_mine, other_core(cot_mine), even, w_out_full)
    hidden_out, d_conv, back = local_call(
        scan_kernel,
        (((rows, channels), bf16), ((rows, channels), f32), ((rows, small_width), bf16)),
        [pltpu.VMEM((rows, channels), f32)] * 5
        + [pltpu.VMEM((rows + 1, a_log.shape[1], channels), f32)],
    )(small, w_dt, dt_bias[None, :], -jnp.exp(a_log).T, d_skip[None, :], conv_out, d_hidden)
    back_chip = pair_sum(back, back)
    (sign_out,) = local_call(
        sign_out_kernel, (((chips, width, channels), bf16),), specs=[inside, inside, left]
    )(hidden_out, cot_whole, back_chip)
    votes_out = along_x(sign_out.reshape(side, side, width, channels)).astype(bf16)
    total = sum_shares(back_chip, sign_out)
    out_parts = local_call(
        out_kernel,
        (((chips, rows, block), f32), ((chips, rows, block), bf16)),
        specs=[inside] * 3 + [left],
    )(hidden_out, w_out_full, even, total)
    back = exchange(total, "tensor", ring).reshape(back_chip.shape)
    d_inner, *grad_parts = local_call(
        grad_kernel,
        (
            ((rows, channels), bf16),
            ((chips, rows, block), f32),
            ((chips, rows, block), bf16),
        ),
        specs=[inside] * 8 + [left] * 2,
    )(back, w_dtlow, w_bc, d_conv, pre, conv_weight, w_in_full, even, votes_out, out_parts[0])
    (sign_in,) = local_call(
        sign_in_kernel, (((side, side, width, channels), bf16),), specs=[inside, inside]
    )(d_inner, whole)
    votes_in = along_y(along_x(sign_in).astype(bf16))
    votes_out = along_y(votes_out)
    (parts,) = local_call(
        pairs_kernel, (((chips, 2 * rows, block), bf16),), specs=[inside] * 4 + [left]
    )(out_parts[0], other_core(out_parts[1]), grad_parts[0], other_core(grad_parts[1]), sign_in)
    sums = jnp.sum(exchange(parts, "tensor", ring).astype(f32), axis=0).astype(bf16)
    merged_in = votes_in / replicas + err_in
    merged_out = votes_out / replicas + err_out
    update_in = jnp.tanh(4.0 * merged_in)
    update_out = jnp.tanh(4.0 * merged_out)
    return (
        sums[:rows],
        sums[rows:],
        update_in,
        merged_in - update_in,
        update_out,
        merged_out - update_out,
    )


def solution(mesh):
    return jax.shard_map(
        on_device,
        mesh=mesh,
        in_specs=(
            P("dp", "tensor"),
            P("dp", "tensor"),
            P(None, "tensor"),
            P("tensor", None),
            P("tensor", None),
            P(None, "tensor"),
            P("tensor"),
            P("tensor", None),
            P("tensor"),
            P("tensor", "dp"),
            P("dp", "tensor"),
            P("dp", "tensor"),
            P("tensor", "dp"),
        ),
        out_specs=(
            P("dp", "tensor"),
            P("dp", "tensor"),
            P("dp", "tensor"),
            P("dp", "tensor"),
            P("tensor", "dp"),
            P("tensor", "dp"),
        ),
        check_vma=False,
    )
```
